32 devices in a mesh: groups: 2 (over y), dp: 4 (over z), shard: 4 (over x, core).
Axes of the slice: x: 2, y: 2, z: 4, core: 2. Of those that a mesh axis runs over, the one named last changes fastest.
Arguments:
- acts: bfloat16 [256, 4096], P(('groups', 'dp'), 'shard'), parts along dimension 0, may hold values from -6 to 6
- grads: bfloat16 [256, 16384], P(('groups', 'dp')), parts along dimension 0, may hold values from -6 to 6
- lengths: int32 [16], P(('groups', 'dp')), parts along dimension 0, may hold values from 1 to 16, 96 in all
- act_basis: bfloat16 [16, 256, 256], P('shard'), may hold values from -0.375 to 0.375
- grad_basis: bfloat16 [64, 256, 256], P('dp'), may hold values from -0.375 to 0.375
- correction: bfloat16 [4096, 16384], P('shard', 'dp'), may hold values from 0.0099487305 to 3
- val_grads: bfloat16 [6, 4096, 16384], P(None, 'shard', 'dp'), may hold values from -9.1552734e-05 to 9.1552734e-05
Outputs:
- scores: float32 [16, 6], P(('groups', 'dp')), parts along dimension 0
- act_cov: float32 [32, 256, 256], P(('groups', 'shard'), 'dp'), parts along dimension 0
- grad_cov: float32 [128, 256, 256], P(('groups', 'dp'), 'shard'), parts along dimension 0
The draws below stay inside these ranges and needn't reach their ends.
There are 2 independent parts, one for each index of `groups`. The reference program is written for one: setup_inputs(seed, part) draws one part's arguments, and reference() takes and returns one part's arrays. A program takes and returns all parts, laid end to end along the dimension named above; an argument that names none is the same for every part. Nothing has to cross between parts.
Inputs may be any that keep to these rules, and one draw needn't show every extreme that they name: lengths[s] counts the real tokens at the start of sequence s, the rest of its 16 slots being padding; the lengths of a pool add up to 96.
All inputs are finite; a program needn't handle non-finite values. No bound on the sum of `lengths` on one device may be relied on, other than what follows from the above.
Results may differ from the reference program's by a relative error of at most 0.008.
Values may be sent and summed in bfloat16 or wider, within the bound.
A program may use at most 192 MiB of HBM per device.

```python
import math
import jax
import jax.numpy as jnp
import numpy as np
from jax import lax

DIN = 4096
DOUT = 16384
BLK = 256
QUERIES = 6
SLEN = 16
TOK_DEV = 32
SEQS = 8
TOKENS = 128
N_DP = 4


def shard_levels(key, extent, pieces, low, largest):
    def one(axis_at, parts):
        draws = jax.random.uniform(jax.random.fold_in(jax.random.fold_in(key, 6), axis_at), (parts,), jnp.float32, low / len(pieces), largest / len(pieces))
        return jnp.repeat(jnp.exp(draws), extent[axis_at] // parts).reshape((-1,) + (1,) * (len(extent) - axis_at - 1))

    level = one(*pieces[0])
    for cut in pieces[1:]:
        level = level * one(*cut)
    return level


def length_profile(count, total, reach, skew):
    weights = [(1 << 20) // math.isqrt(grade ** skew) + 1 for grade in range(2, count + 1)]
    rest, holding = total - reach - (count - 1), [1] * (count - 1)
    while rest > 0:
        candidates = [i for i in range(count - 1) if holding[i] < reach]
        mass, remaining = sum([weights[i] for i in candidates]), rest
        for i in candidates:
            addition = min(reach - holding[i], max(1, remaining * weights[i] // mass), rest)
            holding[i] = holding[i] + addition
            rest = rest - addition
    return np.array([reach] + holding)


def uneven_parts(key, number_of, total, most, slope):
    if number_of == 2:
        one = jax.random.randint(key, (), max(1, total - most), min(most, total - 1) + 1)
        return jnp.stack([one, total - one])
    tallies = jnp.asarray(length_profile(number_of, total, most, slope), jnp.int32)
    pairs = (number_of - 1) // 2
    giver, receiver = tallies[1:1 + 2 * pairs:2], tallies[2:2 + 2 * pairs:2]
    slack = jnp.minimum(giver - 1, most - receiver)
    shifted = jax.random.randint(jax.random.fold_in(key, 1), (pairs,), 0, 1 << 20) % (slack + 1)
    tallies = tallies.at[1:1 + 2 * pairs:2].set(giver - shifted).at[2:2 + 2 * pairs:2].set(receiver + shifted)
    return tallies[jax.random.permutation(jax.random.fold_in(key, 2), number_of)]


def scatter_about(rng, dims, scale, limit, cuts=(), kind=jnp.bfloat16):
    array = jax.random.normal(rng, dims, jnp.float32) * scale
    if len(cuts) > 0:
        array = shard_levels(rng, dims, cuts, -0.22, 0.18) * array
    return jnp.clip(array, min=-limit, max=limit).astype(kind)


def setup_inputs(seed: int = 0, part: int = 0) -> dict:
    keys = jax.random.split(jax.random.key(seed), 8)
    part_splits = jax.random.split(jax.random.fold_in(keys[7], part), 8)
    return {
        "acts": scatter_about(part_splits[0], (TOKENS, DIN), 1.0, 6.0, ((0, 4), (1, 4))),
        "grads": scatter_about(part_splits[1], (TOKENS, DOUT), 1.0, 6.0, ((0, 4),)),
        "lengths": uneven_parts(part_splits[2], SEQS, SEQS * SLEN * 3 // 4, SLEN, 0).astype(jnp.int32),
        "act_basis": scatter_about(keys[3], (DIN // BLK, BLK, BLK), BLK ** -0.5, 0.375, ((0, 4),)),
        "grad_basis": scatter_about(keys[4], (DOUT // BLK, BLK, BLK), BLK ** -0.5, 0.375, ((0, 4),)),
        "correction": jnp.clip(jnp.exp(math.log(3.0) - 5.7089226 * jax.random.uniform(keys[5], (DIN, DOUT), jnp.float32) ** shard_levels(keys[5], (DIN, DOUT), ((0, 4), (1, 4)), -0.2, 0.2)), 0.0099487305, 3.0).astype(jnp.bfloat16),
        "val_grads": scatter_about(keys[6], (QUERIES, DIN, DOUT), (64 * DIN * DOUT) ** -0.5, 9.1552734375e-05, ((1, 4), (2, 4))),
    }


damping = 0.1


def turn_blocks(row_data, eigen_basis):
    row_count = row_data.shape[0]
    block_count = eigen_basis.shape[0]
    blocked = row_data.reshape(row_count, block_count, BLK).astype(jnp.float32)
    rotated = jnp.einsum("tbi,bij->tbj", blocked, eigen_basis.astype(jnp.float32))
    return rotated.reshape(row_count, block_count * BLK).astype(jnp.bfloat16)


def reference(acts, grads, lengths, act_basis, grad_basis, correction, val_grads):
    position = jnp.arange(TOKENS, dtype=jnp.int32) % SLEN
    token_keep = (position < jnp.repeat(lengths, SLEN)).astype(jnp.bfloat16)[:, None]
    act_masked = acts * token_keep
    grad_masked = grads * token_keep
    act_turned = turn_blocks(act_masked, act_basis)
    grad_turned = turn_blocks(grad_masked, grad_basis)
    run_rows = act_masked.reshape(N_DP, TOK_DEV, DIN // BLK, BLK)

    def add_run(running, one_run):
        widened = one_run.astype(jnp.float32)
        run_part = jnp.einsum("tbi,tbj->bij", widened, widened).astype(jnp.bfloat16)
        run_part = lax.optimization_barrier(run_part)
        return running + run_part.astype(jnp.float32), None

    act_sum, unused = lax.scan(add_run, jnp.zeros((DIN // BLK, BLK, BLK), jnp.float32), run_rows)
    act_cov = act_sum / TOKENS
    grad_blocks = grad_masked.reshape(TOKENS, DOUT // BLK, BLK).astype(jnp.float32)
    grad_cov = jnp.einsum("tbi,tbj->bij", grad_blocks, grad_blocks) / TOKENS
    act_wide = act_turned.astype(jnp.float32)
    eigen_values = correction.astype(jnp.float32) + damping

    def score_query(query_grad):
        precond = (query_grad.astype(jnp.float32) / eigen_values).astype(jnp.bfloat16)
        mixed_terms = lax.dot_general(grad_turned, precond, (((1,), (1,)), ((), ())), preferred_element_type=jnp.float32)
        return jnp.sum(mixed_terms * act_wide, axis=1)

    token_scores = lax.map(score_query, val_grads)
    scores = token_scores.reshape(QUERIES, SEQS, SLEN).sum(axis=2).T
    return scores, act_cov, grad_cov
```

```python
import functools

import jax
import jax.numpy as jnp
from jax import lax
from jax.experimental import pallas as pl
from jax.experimental.pallas import tpu as pltpu
from jax.sharding import PartitionSpec as P

damping = 0.1
MESH = pl.DeviceIdType.MESH
MIB = 1 << 20
VMEM_LIMIT = 62 * MIB
STREAM_BYTES = 46 * MIB


def rotate_blocks(row_data, eigen_basis):
    row_count = row_data.shape[0]
    block_count = eigen_basis.shape[0]
    block_width = eigen_basis.shape[1]
    blocked = row_data.reshape(row_count, block_count, block_width)
    rotated = jnp.einsum("tbi,bij->tbj", blocked, eigen_basis, preferred_element_type=jnp.float32)
    return rotated.reshape(row_count, block_count * block_width).astype(jnp.bfloat16)


def block_products(left_rows, right_rows):
    return jnp.einsum("tbi,tbj->bij", left_rows, right_rows, preferred_element_type=jnp.float32)


def local_plain(acts, grads, lengths, act_basis, grad_basis, correction, val_grads):
    n_data = lax.axis_size("dp")
    n_shard = lax.axis_size("shard")
    tok_dev = acts.shape[0]
    seq_len = tok_dev // lengths.shape[0]
    total_tokens = tok_dev * n_data
    block_width = act_basis.shape[1]
    queries = val_grads.shape[0]
    position = jnp.arange(tok_dev, dtype=jnp.int32) % seq_len
    token_keep = (position < jnp.repeat(lengths, seq_len)).astype(jnp.bfloat16)[:, None]
    act_masked = acts * token_keep
    grad_masked = grads * token_keep
    act_turned = rotate_blocks(act_masked, act_basis)
    act_blocks = act_masked.reshape(tok_dev, -1, block_width)
    act_cov = (
        lax.psum_scatter(
            block_products(act_blocks, act_blocks).astype(jnp.bfloat16),
            "dp",
            scatter_dimension=1,
            tiled=True,
        ).astype(jnp.float32)
        / total_tokens
    )
    grad_cols = lax.all_to_all(grad_masked, "dp", split_axis=1, concat_axis=0, tiled=True)
    grad_turned = rotate_blocks(grad_cols, grad_basis)
    grad_blocks = grad_cols.reshape(total_tokens, -1, block_width)
    rows_each = block_width // n_shard
    own_rows = lax.dynamic_slice_in_dim(
        grad_blocks, lax.axis_index("shard") * rows_each, rows_each, 2
    )
    grad_cov = block_products(own_rows, grad_blocks) / total_tokens
    precond = (val_grads.astype(jnp.float32) / (correction.astype(jnp.float32) + damping)).astype(
        jnp.bfloat16
    )
    arrived = lax.all_gather(act_turned, "dp", axis=0, tiled=True)
    row_count = arrived.shape[0]
    mixed_terms = jnp.einsum(
        "tj,qij->tqi", grad_turned, precond, preferred_element_type=jnp.float32
    )
    token_scores = jnp.sum(mixed_terms * arrived.astype(jnp.float32)[:, None, :], axis=2)
    seq_scores = token_scores.reshape(row_count // seq_len, seq_len, queries).sum(axis=1)
    everything = lax.psum(seq_scores, ("dp", "shard"))
    seq_dev = lengths.shape[0]
    scores = lax.dynamic_slice_in_dim(everything, lax.axis_index("dp") * seq_dev, seq_dev, 0)
    return (scores, act_cov, grad_cov)


def kernel(
    n_dp, n_shard, chunk, slots, kstep,
    len_ref, acts_ref, grads_ref, abasis_ref, gbasis_ref, corr_ref, val_ref,
    scores_ref, acov_ref, gcov_ref,
    gbuf, gsend, abuf, abasis, gbasis, g_t, a_t, turn, val_buf, corr_buf, acc, red_dp, red_sh,
    own_sem, out_sem, act_sem, ab_sem, gb_sem, val_sem, corr_sem,
    gsend_sem, grecv_sem, asend_sem, arecv_sem, fx_sem, fc_sem, fr_sem,
    rds_sem, rdr_sem, rss_sem, rsr_sem,
):
    d = lax.axis_index("dp")
    s = lax.axis_index("shard")
    tok = acts_ref.shape[0]
    n_seq = len_ref.shape[0]
    seq_len = tok // n_seq
    tokens = tok * n_dp
    blk = abasis_ref.shape[1]
    a_blocks = abasis_ref.shape[0]
    g_blocks = gbasis_ref.shape[0]
    queries, rows, cols = val_ref.shape
    part = cols // n_shard
    part_blocks = part // blk
    chunks = rows // chunk

    other_core = s + 1 - 2 * lax.rem(s, 2)
    other_chip = lax.rem(s + 2, 4)
    across = other_core + 2 - 4 * (other_core // 2)
    peers = [lax.rem(d + k, n_dp) for k in range(1, n_dp)]

    def own_copy(j):
        start = pl.multiple_of(d * cols + j * part, part)
        return pltpu.make_async_copy(grads_ref.at[:, pl.ds(start, part)], gbuf.at[j, d], own_sem.at[j])

    def out_copy(k):
        start = pl.multiple_of(peers[k] * cols + s * part, part)
        return pltpu.make_async_copy(grads_ref.at[:, pl.ds(start, part)], gsend.at[k], out_sem.at[k])

    act_copy = pltpu.make_async_copy(acts_ref, abuf.at[d], act_sem)
    abasis_copy = pltpu.make_async_copy(abasis_ref, abasis, ab_sem)
    gbasis_copy = pltpu.make_async_copy(gbasis_ref, gbasis, gb_sem)

    def val_copy(c, slot):
        at = pl.multiple_of(c * chunk, chunk)
        return pltpu.make_async_copy(val_ref.at[:, pl.ds(at, chunk), :], val_buf.at[slot], val_sem.at[slot])

    def corr_copy(c, slot):
        at = pl.multiple_of(c * chunk, chunk)
        return pltpu.make_async_copy(corr_ref.at[pl.ds(at, chunk), :], corr_buf.at[slot], corr_sem.at[slot])

    for k in range(n_dp - 1):
        out_copy(k).start()
    act_copy.start()
    for j in range(n_shard):
        own_copy(j).start()
    gbasis_copy.start()
    abasis_copy.start()

    @pl.loop(0, slots)
    def _(c):
        corr_copy(c, c).start()
        val_copy(c, c).start()

    barrier = pltpu.get_barrier_semaphore()
    for p in peers:
        pl.semaphore_signal(barrier, inc=1, device_id={"dp": p}, device_id_type=MESH)
    for p in (other_core, other_chip, across):
        pl.semaphore_signal(barrier, inc=1, device_id={"shard": p}, device_id_type=MESH)

    row_at = lax.broadcasted_iota(jnp.int32, (tok, part), 0)
    limit = jnp.zeros((tok, part), jnp.int32)
    for q in range(n_seq):
        limit = jnp.where(row_at // seq_len == q, len_ref[q], limit)
    keep = lax.rem(row_at, seq_len) < limit

    def masked(x):
        return jnp.where(keep, x.astype(jnp.float32), 0.0).astype(jnp.bfloat16)

    for k in range(n_dp - 1):
        out_copy(k).wait()
        gsend[k] = masked(gsend[k])

    pl.semaphore_wait(barrier, n_dp - 1 + 3)

    def grad_send(k):
        return pltpu.make_async_remote_copy(
            gsend.at[k], gbuf.at[s, d], gsend_sem.at[k], grecv_sem.at[s, d],
            device_id={"dp": peers[k]}, device_id_type=MESH)

    def grad_arrival(j, p):
        return pltpu.make_async_remote_copy(
            gsend.at[0], gbuf.at[j, p], gsend_sem.at[0], grecv_sem.at[j, p],
            device_id={"dp": peers[0]}, device_id_type=MESH)

    order = [0, n_dp - 2] + list(range(1, n_dp - 2)) if n_dp > 2 else list(range(n_dp - 1))
    for k in order:
        grad_send(k).start()

    act_copy.wait()
    for j in range(abuf.shape[2] // part):
        abuf[d, :, j * part:(j + 1) * part] = masked(abuf[d, :, j * part:(j + 1) * part])

    def act_send(k):
        return pltpu.make_async_remote_copy(
            abuf.at[d], abuf.at[d], asend_sem.at[k], arecv_sem.at[d],
            device_id={"dp": peers[k]}, device_id_type=MESH)

    def act_arrival(p):
        return pltpu.make_async_remote_copy(
            abuf.at[d], abuf.at[p], asend_sem.at[0], arecv_sem.at[p],
            device_id={"dp": peers[0]}, device_id_type=MESH)

    for k in order:
        act_send(k).start()

    for j in range(n_shard):
        own_copy(j).wait()
        gbuf[j, d] = masked(gbuf[j, d])

    def pass_on(k, j, sems, target):
        p = peers[k]
        return pltpu.make_async_remote_copy(
            gbuf.at[j, p], gbuf.at[j, p], sems.at[k], grecv_sem.at[j, p],
            device_id={"shard": target}, device_id_type=MESH)

    for k in order:
        grad_arrival(s, peers[k]).wait_recv()
        pass_on(k, s, fx_sem, other_chip).start()
        pass_on(k, s, fc_sem, other_core).start()

    gbasis_copy.wait()

    def turn_part(j):
        x = gbuf[j].reshape(tokens, part)
        for b in range(part_blocks):
            y = jnp.dot(x[:, b * blk:(b + 1) * blk], gbasis[j * part_blocks + b],
                        preferred_element_type=jnp.float32)
            at = pl.multiple_of((j * part_blocks + b) * blk, blk)
            g_t[pl.ds(at, blk), :] = y.T.astype(jnp.bfloat16)

    turn_part(s)
    for k in order:
        grad_arrival(other_chip, peers[k]).wait_recv()
        pass_on(k, other_chip, fr_sem, other_core).start()
    turn_part(other_chip)
    for k in order:
        grad_arrival(other_core, peers[k]).wait_recv()
    turn_part(other_core)
    for k in order:
        grad_arrival(across, peers[k]).wait_recv()
    turn_part(across)

    abasis_copy.wait()
    for k in order:
        act_arrival(peers[k]).wait_recv()
    for b in range(a_blocks):
        x = abuf[:, :, b * blk:(b + 1) * blk].reshape(tokens, blk)
        y = jnp.dot(x, abasis[b], preferred_element_type=jnp.float32)
        a_t[b * blk:(b + 1) * blk, :] = y.astype(jnp.bfloat16).astype(jnp.float32).T

    acc[...] = jnp.zeros_like(acc)

    @pl.loop(0, chunks)
    def _(c):
        slot = lax.rem(c, slots)
        corr_copy(c, slot).wait()
        val_copy(c, slot).wait()

        def column_step(j, sums):
            at = pl.multiple_of(j * kstep, kstep)
            inverse = 1.0 / (corr_buf[slot, :, pl.ds(at, kstep)].astype(jnp.float32) + damping)
            right = g_t[pl.ds(at, kstep), :]
            out = []
            for q in range(queries):
                pre = (val_buf[slot, q, :, pl.ds(at, kstep)].astype(jnp.float32) * inverse).astype(jnp.bfloat16)
                out.append(sums[q] + jnp.dot(pre, right, preferred_element_type=jnp.float32))
            return tuple(out)

        zero = jnp.zeros((chunk, tokens), jnp.float32)
        sums = lax.fori_loop(0, cols // kstep, column_step, (zero,) * queries)
        weight = a_t[pl.ds(pl.multiple_of(c * chunk, chunk), chunk), :]
        for q in range(queries):
            acc[q] += jnp.sum((sums[q] * weight).reshape(chunk // 8, 8, tokens), axis=0)

        @pl.when(c + slots < chunks)
        def _():
            corr_copy(c + slots, slot).start()
            val_copy(c + slots, slot).start()

    for q in range(queries):
        red_dp[d, q:q + 1, :] = jnp.sum(acc[q], axis=0, keepdims=True)
    red_dp[d, queries:, :] = jnp.zeros((8 - queries, tokens), jnp.float32)

    def dp_send(k):
        return pltpu.make_async_remote_copy(
            red_dp.at[d], red_dp.at[d], rds_sem.at[k], rdr_sem.at[d],
            device_id={"dp": peers[k]}, device_id_type=MESH)

    def dp_arrival(k):
        return pltpu.make_async_remote_copy(
            red_dp.at[d], red_dp.at[peers[k]], rds_sem.at[k], rdr_sem.at[peers[k]],
            device_id={"dp": peers[k]}, device_id_type=MESH)

    for k in range(n_dp - 1):
        dp_send(k).start()

    a_rows = blk // n_dp
    lane = lax.broadcasted_iota(jnp.int32, (a_rows, tokens), 1)
    for b in range(a_blocks):
        x = abuf[:, :, b * blk:(b + 1) * blk].reshape(tokens, blk)
        turn[b] = x.astype(jnp.float32).T
        left = turn[b, pl.ds(pl.multiple_of(d * a_rows, a_rows), a_rows), :]
        total = jnp.zeros((a_rows, blk), jnp.float32)
        for r in range(n_dp):
            run = jnp.where(lane // tok == r, left, 0.0).astype(jnp.bfloat16)
            total += jnp.dot(run, x, preferred_element_type=jnp.float32).astype(jnp.bfloat16).astype(jnp.float32)
        acov_ref[b] = total / tokens

    for k in range(n_dp - 1):
        dp_arrival(k).wait_recv()
    total = red_dp[0]
    for p in range(1, n_dp):
        total += red_dp[p]
    red_sh[s] = total

    others = (other_core, other_chip, across)

    def sh_send(k):
        return pltpu.make_async_remote_copy(
            red_sh.at[s], red_sh.at[s], rss_sem.at[k], rsr_sem.at[s],
            device_id={"shard": others[k]}, device_id_type=MESH)

    def sh_arrival(k):
        return pltpu.make_async_remote_copy(
            red_sh.at[s], red_sh.at[others[k]], rss_sem.at[k], rsr_sem.at[others[k]],
            device_id={"shard": others[k]}, device_id_type=MESH)

    for k in range(3):
        sh_send(k).start()

    g_rows = blk // n_shard
    for j in range(n_shard):
        for b in range(part_blocks):
            at = b % turn.shape[0]
            x = gbuf[j, :, :, b * blk:(b + 1) * blk].reshape(tokens, blk)
            turn[at] = x.astype(jnp.float32).T
            left = turn[at, pl.ds(pl.multiple_of(s * g_rows, g_rows), g_rows), :].astype(jnp.bfloat16)
            gcov_ref[j * part_blocks + b] = jnp.dot(left, x, preferred_element_type=jnp.float32) / tokens

    for k in range(3):
        sh_arrival(k).wait_recv()
    total = red_sh[0]
    for p in range(1, n_shard):
        total += red_sh[p]
    lane = lax.broadcasted_iota(jnp.int32, (8, tokens), 1)
    row = lax.broadcasted_iota(jnp.int32, (8, tokens), 0)
    for q in range(n_seq):
        one = jnp.sum(jnp.where(lane // seq_len == d * n_seq + q, total, 0.0), axis=1, keepdims=True)
        line = jnp.sum(jnp.where(lane == row, one, 0.0), axis=0, keepdims=True)
        scores_ref[q:q + 1, :] = line[:, :queries]

    for k in range(n_dp - 1):
        grad_send(k).wait_send()
        act_send(k).wait_send()
        pass_on(k, s, fx_sem, other_chip).wait_send()
        pass_on(k, s, fc_sem, other_core).wait_send()
        pass_on(k, other_chip, fr_sem, other_core).wait_send()
        dp_send(k).wait_send()
    for k in range(3):
        sh_send(k).wait_send()


def fits(n_dp, n_shard, acts, lengths, act_basis, grad_basis, val_grads):
    tok = acts.shape[0]
    blk = act_basis.shape[1]
    queries, rows, cols = val_grads.shape
    return (
        n_shard == 4 and tok * n_dp == 128 and tok % 16 == 0 and queries <= 7
        and tok % lengths.shape[0] == 0 and blk % 128 == 0
        and blk % (16 * n_dp) == 0 and blk % (16 * n_shard) == 0
        and cols % (blk * n_shard) == 0 and rows % (cols // n_shard) == 0 and rows % 64 == 0
    )


def local(acts, grads, lengths, act_basis, grad_basis, correction, val_grads):
    n_dp = lax.axis_size("dp")
    n_shard = lax.axis_size("shard")
    if not fits(n_dp, n_shard, acts, lengths, act_basis, grad_basis, val_grads):
        return local_plain(acts, grads, lengths, act_basis, grad_basis, correction, val_grads)
    tok = acts.shape[0]
    tokens = tok * n_dp
    blk = act_basis.shape[1]
    a_blocks, g_blocks = act_basis.shape[0], grad_basis.shape[0]
    queries, rows, cols = val_grads.shape
    part = cols // n_shard
    chunk = 64
    slots = min(rows // chunk, STREAM_BYTES // ((queries + 1) * chunk * cols * 2))
    kstep = min(512, cols)
    dma = pltpu.SemaphoreType.DMA
    bf16, f32 = jnp.bfloat16, jnp.float32
    anywhere = pl.BlockSpec(memory_space=pl.ANY)
    vmem = pl.BlockSpec(memory_space=pltpu.VMEM)
    return pl.pallas_call(
        functools.partial(kernel, n_dp, n_shard, chunk, slots, kstep),
        out_shape=(
            jax.ShapeDtypeStruct((lengths.shape[0], queries), f32),
            jax.ShapeDtypeStruct((a_blocks, blk // n_dp, blk), f32),
            jax.ShapeDtypeStruct((g_blocks, blk // n_shard, blk), f32),
        ),
        in_specs=[pl.BlockSpec(memory_space=pltpu.SMEM)] + [anywhere] * 6,
        out_specs=(vmem, vmem, vmem),
        scratch_shapes=[
            pltpu.VMEM((n_shard, n_dp, tok, part), bf16),
            pltpu.VMEM((n_dp - 1, tok, part), bf16),
            pltpu.VMEM((n_dp, tok, rows), bf16),
            pltpu.VMEM((a_blocks, blk, blk), bf16),
            pltpu.VMEM((g_blocks, blk, blk), bf16),
            pltpu.VMEM((cols, tokens), bf16),
            pltpu.VMEM((rows, tokens), f32),
            pltpu.VMEM((max(a_blocks, 2), blk, tokens), f32),
            pltpu.VMEM((slots, queries, chunk, cols), bf16),
            pltpu.VMEM((slots, chunk, cols), bf16),
            pltpu.VMEM((queries, 8, tokens), f32),
            pltpu.VMEM((n_dp, 8, tokens), f32),
            pltpu.VMEM((n_shard, 8, tokens), f32),
            dma((n_shard,)), dma((n_dp - 1,)), dma(()), dma(()), dma(()), dma((slots,)), dma((slots,)),
            dma((n_dp - 1,)), dma((n_shard, n_dp)), dma((n_dp - 1,)), dma((n_dp,)),
            dma((n_dp - 1,)), dma((n_dp - 1,)), dma((n_dp - 1,)),
            dma((n_dp - 1,)), dma((n_dp,)), dma((3,)), dma((n_shard,)),
        ],
        compiler_params=pltpu.CompilerParams(
            collective_id=0, has_side_effects=True, vmem_limit_bytes=VMEM_LIMIT
        ),
        name="scores_and_covariances",
    )(lengths, acts, grads, act_basis, grad_basis, correction, val_grads)


def solution(mesh):
    in_specs = (
        P(("groups", "dp"), "shard"),
        P(("groups", "dp"), None),
        P(("groups", "dp")),
        P("shard", None, None),
        P("dp", None, None),
        P("shard", "dp"),
        P(None, "shard", "dp"),
    )
    out_specs = (
        P(("groups", "dp"), None),
        P(("groups", "shard"), "dp", None),
        P(("groups", "dp"), "shard", None),
    )
    return jax.shard_map(local, mesh=mesh, in_specs=in_specs, out_specs=out_specs, check_vma=False)
```

```python
import functools

import jax
import jax.numpy as jnp
from jax import lax
from jax.experimental import pallas as pl
from jax.experimental.pallas import tpu as pltpu
from jax.sharding import PartitionSpec as P

damping = 0.1
MESH = pl.DeviceIdType.MESH
MIB = 1 << 20
VMEM_LIMIT = 62 * MIB
STREAM_BYTES = 46 * MIB


def rotate_blocks(row_data, eigen_basis):
    row_count = row_data.shape[0]
    block_count = eigen_basis.shape[0]
    block_width = eigen_basis.shape[1]
    blocked = row_data.reshape(row_count, block_count, block_width)
    rotated = jnp.einsum("tbi,bij->tbj", blocked, eigen_basis, preferred_element_type=jnp.float32)
    return rotated.reshape(row_count, block_count * block_width).astype(jnp.bfloat16)


def block_products(left_rows, right_rows):
    return jnp.einsum("tbi,tbj->bij", left_rows, right_rows, preferred_element_type=jnp.float32)


def local_plain(acts, grads, lengths, act_basis, grad_basis, correction, val_grads):
    n_data = lax.axis_size("dp")
    n_shard = lax.axis_size("shard")
    tok_dev = acts.shape[0]
    seq_len = tok_dev // lengths.shape[0]
    total_tokens = tok_dev * n_data
    block_width = act_basis.shape[1]
    queries = val_grads.shape[0]
    position = jnp.arange(tok_dev, dtype=jnp.int32) % seq_len
    token_keep = (position < jnp.repeat(lengths, seq_len)).astype(jnp.bfloat16)[:, None]
    act_masked = acts * token_keep
    grad_masked = grads * token_keep
    act_turned = rotate_blocks(act_masked, act_basis)
    act_blocks = act_masked.reshape(tok_dev, -1, block_width)
    act_cov = (
        lax.psum_scatter(
            block_products(act_blocks, act_blocks).astype(jnp.bfloat16),
            "dp",
            scatter_dimension=1,
            tiled=True,
        ).astype(jnp.float32)
        / total_tokens
    )
    grad_cols = lax.all_to_all(grad_masked, "dp", split_axis=1, concat_axis=0, tiled=True)
    grad_turned = rotate_blocks(grad_cols, grad_basis)
    grad_blocks = grad_cols.reshape(total_tokens, -1, block_width)
    rows_each = block_width // n_shard
    own_rows = lax.dynamic_slice_in_dim(
        grad_blocks, lax.axis_index("shard") * rows_each, rows_each, 2
    )
    grad_cov = block_products(own_rows, grad_blocks) / total_tokens
    precond = (val_grads.astype(jnp.float32) / (correction.astype(jnp.float32) + damping)).astype(
        jnp.bfloat16
    )
    arrived = lax.all_gather(act_turned, "dp", axis=0, tiled=True)
    row_count = arrived.shape[0]
    mixed_terms = jnp.einsum(
        "tj,qij->tqi", grad_turned, precond, preferred_element_type=jnp.float32
    )
    token_scores = jnp.sum(mixed_terms * arrived.astype(jnp.float32)[:, None, :], axis=2)
    seq_scores = token_scores.reshape(row_count // seq_len, seq_len, queries).sum(axis=1)
    everything = lax.psum(seq_scores, ("dp", "shard"))
    seq_dev = lengths.shape[0]
    scores = lax.dynamic_slice_in_dim(everything, lax.axis_index("dp") * seq_dev, seq_dev, 0)
    return (scores, act_cov, grad_cov)


def kernel(
    n_dp, n_shard, chunk, slots, kstep,
    len_ref, acts_ref, grads_ref, abasis_ref, gbasis_ref, corr_ref, val_ref,
    scores_ref, acov_ref, gcov_ref,
    gbuf, gsend, abuf, abasis, gbasis, g_t, a_t, turn, val_buf, corr_buf, acc, red_dp, red_sh,
    own_sem, out_sem, act_sem, ab_sem, gb_sem, val_sem, corr_sem,
    gsend_sem, grecv_sem, asend_sem, arecv_sem, fx_sem, fc_sem, fr_sem,
    rds_sem, rdr_sem, rss_sem, rsr_sem,
):
    d = lax.axis_index("dp")
    s = lax.axis_index("shard")
    tok = acts_ref.shape[0]
    n_seq = len_ref.shape[0]
    seq_len = tok // n_seq
    tokens = tok * n_dp
    blk = abasis_ref.shape[1]
    a_blocks = abasis_ref.shape[0]
    g_blocks = gbasis_ref.shape[0]
    queries, rows, cols = val_ref.shape
    part = cols // n_shard
    part_blocks = part // blk
    chunks = rows // chunk

    other_core = s + 1 - 2 * lax.rem(s, 2)
    other_chip = lax.rem(s + 2, 4)
    across = other_core + 2 - 4 * (other_core // 2)
    peers = [lax.rem(d + k, n_dp) for k in range(1, n_dp)]

    def own_copy(j):
        start = pl.multiple_of(d * cols + j * part, part)
        return pltpu.make_async_copy(grads_ref.at[:, pl.ds(start, part)], gbuf.at[j, d], own_sem.at[j])

    def out_copy(k):
        start = pl.multiple_of(peers[k] * cols + s * part, part)
        return pltpu.make_async_copy(grads_ref.at[:, pl.ds(start, part)], gsend.at[k], out_sem.at[k])

    act_copy = pltpu.make_async_copy(acts_ref, abuf.at[d], act_sem)
    abasis_copy = pltpu.make_async_copy(abasis_ref, abasis, ab_sem)
    gbasis_copy = pltpu.make_async_copy(gbasis_ref, gbasis, gb_sem)

    def val_copy(c, slot):
        at = pl.multiple_of(c * chunk, chunk)
        return pltpu.make_async_copy(val_ref.at[:, pl.ds(at, chunk), :], val_buf.at[slot], val_sem.at[slot])

    def corr_copy(c, slot):
        at = pl.multiple_of(c * chunk, chunk)
        return pltpu.make_async_copy(corr_ref.at[pl.ds(at, chunk), :], corr_buf.at[slot], corr_sem.at[slot])

    barrier = pltpu.get_barrier_semaphore()
    for p in peers:
        pl.semaphore_signal(barrier, inc=1, device_id={"dp": p}, device_id_type=MESH)
    for p in (other_core, other_chip, across):
        pl.semaphore_signal(barrier, inc=1, device_id={"shard": p}, device_id_type=MESH)

    for k in range(n_dp - 1):
        out_copy(k).start()
    act_copy.start()
    for j in range(n_shard):
        own_copy(j).start()
    gbasis_copy.start()
    abasis_copy.start()

    @pl.loop(0, slots)
    def _(c):
        corr_copy(c, c).start()
        val_copy(c, c).start()

    row_at = lax.broadcasted_iota(jnp.int32, (tok, part), 0)
    limit = jnp.zeros((tok, part), jnp.int32)
    for q in range(n_seq):
        limit = jnp.where(row_at // seq_len == q, len_ref[q], limit)
    keep = lax.rem(row_at, seq_len) < limit

    def masked(x):
        return jnp.where(keep, x.astype(jnp.float32), 0.0).astype(jnp.bfloat16)

    for k in range(n_dp - 1):
        out_copy(k).wait()
        gsend[k] = masked(gsend[k])

    pl.semaphore_wait(barrier, n_dp - 1 + 3)

    def grad_send(k):
        return pltpu.make_async_remote_copy(
            gsend.at[k], gbuf.at[s, d], gsend_sem.at[k], grecv_sem.at[s, d],
            device_id={"dp": peers[k]}, device_id_type=MESH)

    def grad_arrival(j, p):
        return pltpu.make_async_remote_copy(
            gsend.at[0], gbuf.at[j, p], gsend_sem.at[0], grecv_sem.at[j, p],
            device_id={"dp": peers[0]}, device_id_type=MESH)

    order = [0, n_dp - 2] + list(range(1, n_dp - 2)) if n_dp > 2 else list(range(n_dp - 1))
    for k in order:
        grad_send(k).start()

    act_copy.wait()
    for j in range(abuf.shape[2] // part):
        abuf[d, :, j * part:(j + 1) * part] = masked(abuf[d, :, j * part:(j + 1) * part])

    def act_send(k):
        return pltpu.make_async_remote_copy(
            abuf.at[d], abuf.at[d], asend_sem.at[k], arecv_sem.at[d],
            device_id={"dp": peers[k]}, device_id_type=MESH)

    def act_arrival(p):
        return pltpu.make_async_remote_copy(
            abuf.at[d], abuf.at[p], asend_sem.at[0], arecv_sem.at[p],
            device_id={"dp": peers[0]}, device_id_type=MESH)

    for k in order:
        act_send(k).start()

    for j in range(n_shard):
        own_copy(j).wait()
        gbuf[j, d] = masked(gbuf[j, d])

    def pass_on(k, j, sems, target):
        p = peers[k]
        return pltpu.make_async_remote_copy(
            gbuf.at[j, p], gbuf.at[j, p], sems.at[k], grecv_sem.at[j, p],
            device_id={"shard": target}, device_id_type=MESH)

    for k in order:
        grad_arrival(s, peers[k]).wait_recv()
        pass_on(k, s, fx_sem, other_chip).start()
        pass_on(k, s, fc_sem, other_core).start()

    gbasis_copy.wait()

    def turn_part(j):
        x = gbuf[j].reshape(tokens, part)
        for b in range(part_blocks):
            y = jnp.dot(x[:, b * blk:(b + 1) * blk], gbasis[j * part_blocks + b],
                        preferred_element_type=jnp.float32)
            at = pl.multiple_of((j * part_blocks + b) * blk, blk)
            g_t[pl.ds(at, blk), :] = y.T.astype(jnp.bfloat16)

    turn_part(s)
    for k in order:
        grad_arrival(other_chip, peers[k]).wait_recv()
        pass_on(k, other_chip, fr_sem, other_core).start()
    turn_part(other_chip)
    for k in order:
        grad_arrival(other_core, peers[k]).wait_recv()
    turn_part(other_core)
    for k in order:
        grad_arrival(across, peers[k]).wait_recv()
    turn_part(across)

    abasis_copy.wait()
    for k in order:
        act_arrival(peers[k]).wait_recv()
    for b in range(a_blocks):
        x = abuf[:, :, b * blk:(b + 1) * blk].reshape(tokens, blk)
        y = jnp.dot(x, abasis[b], preferred_element_type=jnp.float32)
        a_t[b * blk:(b + 1) * blk, :] = y.astype(jnp.bfloat16).astype(jnp.float32).T

    acc[...] = jnp.zeros_like(acc)

    @pl.loop(0, chunks)
    def _(c):
        slot = lax.rem(c, slots)
        corr_copy(c, slot).wait()
        val_copy(c, slot).wait()

        def column_step(j, sums):
            at = j * kstep
            inverse = 1.0 / (corr_buf[slot, :, pl.ds(at, kstep)].astype(jnp.float32) + damping)
            right = g_t[pl.ds(at, kstep), :]
            pre = [
                (val_buf[slot, q, :, pl.ds(at, kstep)].astype(jnp.float32) * inverse).astype(jnp.bfloat16)
                for q in range(queries)
            ]
            return sums + jnp.dot(jnp.concatenate(pre, axis=0), right, preferred_element_type=jnp.float32)

        sums = jnp.zeros((queries * chunk, tokens), jnp.float32)
        for j in range(cols // kstep):
            sums = column_step(j, sums)
        weight = a_t[pl.ds(pl.multiple_of(c * chunk, chunk), chunk), :]
        for q in range(queries):
            acc[q] += jnp.sum((sums[q * chunk:(q + 1) * chunk] * weight).reshape(chunk // 8, 8, tokens), axis=0)

        @pl.when(c + slots < chunks)
        def _():
            corr_copy(c + slots, slot).start()
            val_copy(c + slots, slot).start()

    for q in range(queries):
        red_dp[d, q:q + 1, :] = jnp.sum(acc[q], axis=0, keepdims=True)
    red_dp[d, queries:, :] = jnp.zeros((8 - queries, tokens), jnp.float32)

    def dp_send(k):
        return pltpu.make_async_remote_copy(
            red_dp.at[d], red_dp.at[d], rds_sem.at[k], rdr_sem.at[d],
            device_id={"dp": peers[k]}, device_id_type=MESH)

    def dp_arrival(k):
        return pltpu.make_async_remote_copy(
            red_dp.at[d], red_dp.at[peers[k]], rds_sem.at[k], rdr_sem.at[peers[k]],
            device_id={"dp": peers[k]}, device_id_type=MESH)

    for k in range(n_dp - 1):
        dp_send(k).start()

    a_rows = blk // n_dp
    lane = lax.broadcasted_iota(jnp.int32, (a_rows, tokens), 1)
    for b in range(a_blocks):
        x = abuf[:, :, b * blk:(b + 1) * blk].reshape(tokens, blk)
        turn[b] = x.astype(jnp.float32).T
        left = turn[b, pl.ds(pl.multiple_of(d * a_rows, a_rows), a_rows), :]
        total = jnp.zeros((a_rows, blk), jnp.float32)
        for r in range(n_dp):
            run = jnp.where(lane // tok == r, left, 0.0).astype(jnp.bfloat16)
            total += jnp.dot(run, x, preferred_element_type=jnp.float32).astype(jnp.bfloat16).astype(jnp.float32)
        acov_ref[b] = total / tokens

    for k in range(n_dp - 1):
        dp_arrival(k).wait_recv()
    total = red_dp[0]
    for p in range(1, n_dp):
        total += red_dp[p]
    red_sh[s] = total

    others = (other_core, other_chip, across)

    def sh_send(k):
        return pltpu.make_async_remote_copy(
            red_sh.at[s], red_sh.at[s], rss_sem.at[k], rsr_sem.at[s],
            device_id={"shard": others[k]}, device_id_type=MESH)

    def sh_arrival(k):
        return pltpu.make_async_remote_copy(
            red_sh.at[s], red_sh.at[others[k]], rss_sem.at[k], rsr_sem.at[others[k]],
            device_id={"shard": others[k]}, device_id_type=MESH)

    for k in range(3):
        sh_send(k).start()

    g_rows = blk // n_shard
    for j in range(n_shard):
        for b in range(part_blocks):
            at = b % turn.shape[0]
            x = gbuf[j, :, :, b * blk:(b + 1) * blk].reshape(tokens, blk)
            turn[at] = x.astype(jnp.float32).T
            left = turn[at, pl.ds(pl.multiple_of(s * g_rows, g_rows), g_rows), :].astype(jnp.bfloat16)
            gcov_ref[j * part_blocks + b] = jnp.dot(left, x, preferred_element_type=jnp.float32) / tokens

    for k in range(3):
        sh_arrival(k).wait_recv()
    total = red_sh[0]
    for p in range(1, n_shard):
        total += red_sh[p]
    lane = lax.broadcasted_iota(jnp.int32, (8, tokens), 1)
    row = lax.broadcasted_iota(jnp.int32, (8, tokens), 0)
    for q in range(n_seq):
        one = jnp.sum(jnp.where(lane // seq_len == d * n_seq + q, total, 0.0), axis=1, keepdims=True)
        line = jnp.sum(jnp.where(lane == row, one, 0.0), axis=0, keepdims=True)
        scores_ref[q:q + 1, :] = line[:, :queries]

    for k in range(n_dp - 1):
        grad_send(k).wait_send()
        act_send(k).wait_send()
        pass_on(k, s, fx_sem, other_chip).wait_send()
        pass_on(k, s, fc_sem, other_core).wait_send()
        pass_on(k, other_chip, fr_sem, other_core).wait_send()
        dp_send(k).wait_send()
    for k in range(3):
        sh_send(k).wait_send()


def hand_on(a, b, c, x, y, z):
    x[...] = a[...]
    y[...] = b[...]
    z[...] = c[...]


def fits(n_dp, n_shard, acts, lengths, act_basis, grad_basis, val_grads):
    tok = acts.shape[0]
    blk = act_basis.shape[1]
    queries, rows, cols = val_grads.shape
    return (
        n_shard == 4 and tok * n_dp == 128 and tok % 16 == 0 and queries <= 7
        and tok % lengths.shape[0] == 0 and blk % 128 == 0
        and blk % (16 * n_dp) == 0 and blk % (16 * n_shard) == 0
        and cols % (blk * n_shard) == 0 and rows % (cols // n_shard) == 0 and rows % 128 == 0
    )


def local(acts, grads, lengths, act_basis, grad_basis, correction, val_grads):
    n_dp = lax.axis_size("dp")
    n_shard = lax.axis_size("shard")
    if not fits(n_dp, n_shard, acts, lengths, act_basis, grad_basis, val_grads):
        return local_plain(acts, grads, lengths, act_basis, grad_basis, correction, val_grads)
    tok = acts.shape[0]
    tokens = tok * n_dp
    blk = act_basis.shape[1]
    a_blocks, g_blocks = act_basis.shape[0], grad_basis.shape[0]
    queries, rows, cols = val_grads.shape
    part = cols // n_shard
    chunk = 128
    slots = min(rows // chunk, STREAM_BYTES // ((queries + 1) * chunk * cols * 2))
    kstep = min(1024, cols)
    dma = pltpu.SemaphoreType.DMA
    bf16, f32 = jnp.bfloat16, jnp.float32
    anywhere = pl.BlockSpec(memory_space=pl.ANY)
    vmem = pl.BlockSpec(memory_space=pltpu.VMEM)
    results = pl.pallas_call(
        functools.partial(kernel, n_dp, n_shard, chunk, slots, kstep),
        out_shape=(
            jax.ShapeDtypeStruct((lengths.shape[0], queries), f32),
            jax.ShapeDtypeStruct((a_blocks, blk // n_dp, blk), f32),
            jax.ShapeDtypeStruct((g_blocks, blk // n_shard, blk), f32),
        ),
        in_specs=[pl.BlockSpec(memory_space=pltpu.SMEM)] + [anywhere] * 6,
        out_specs=(vmem, vmem, vmem),
        scratch_shapes=[
            pltpu.VMEM((n_shard, n_dp, tok, part), bf16),
            pltpu.VMEM((n_dp - 1, tok, part), bf16),
            pltpu.VMEM((n_dp, tok, rows), bf16),
            pltpu.VMEM((a_blocks, blk, blk), bf16),
            pltpu.VMEM((g_blocks, blk, blk), bf16),
            pltpu.VMEM((cols, tokens), bf16),
            pltpu.VMEM((rows, tokens), f32),
            pltpu.VMEM((max(a_blocks, 2), blk, tokens), f32),
            pltpu.VMEM((slots, queries, chunk, cols), bf16),
            pltpu.VMEM((slots, chunk, cols), bf16),
            pltpu.VMEM((queries, 8, tokens), f32),
            pltpu.VMEM((n_dp, 8, tokens), f32),
            pltpu.VMEM((n_shard, 8, tokens), f32),
            dma((n_shard,)), dma((n_dp - 1,)), dma(()), dma(()), dma(()), dma((slots,)), dma((slots,)),
            dma((n_dp - 1,)), dma((n_shard, n_dp)), dma((n_dp - 1,)), dma((n_dp,)),
            dma((n_dp - 1,)), dma((n_dp - 1,)), dma((n_dp - 1,)),
            dma((n_dp - 1,)), dma((n_dp,)), dma((3,)), dma((n_shard,)),
        ],
        compiler_params=pltpu.CompilerParams(
            collective_id=0, has_side_effects=True, vmem_limit_bytes=VMEM_LIMIT
        ),
        name="scores_and_covariances",
    )(lengths, acts, grads, act_basis, grad_basis, correction, val_grads)
    return pl.pallas_call(
        hand_on,
        out_shape=tuple(jax.ShapeDtypeStruct(r.shape, r.dtype) for r in results),
        in_specs=[vmem] * 3,
        out_specs=(vmem,) * 3,
        name="hand_on_results",
    )(*results)


def solution(mesh):
    in_specs = (
        P(("groups", "dp"), "shard"),
        P(("groups", "dp"), None),
        P(("groups", "dp")),
        P("shard", None, None),
        P("dp", None, None),
        P("shard", "dp"),
        P(None, "shard", "dp"),
    )
    out_specs = (
        P(("groups", "dp"), None),
        P(("groups", "shard"), "dp", None),
        P(("groups", "dp"), "shard", None),
    )
    return jax.shard_map(local, mesh=mesh, in_specs=in_specs, out_specs=out_specs, check_vma=False)
```
